512 devices in a mesh: mem: 32 (over z_hi, y, x), tile: 16 (over z_lo, core).
Axes of the slice: x: 4, y: 4, z: 16 (z_hi: 2, z_lo: 8; z = z_hi * 8 + z_lo), core: 2. Of those that a mesh axis runs over, the one named last changes fastest.
Arguments:
- ensemble_state: bfloat16 [128, 32, 128, 768], P('mem', 'tile'), may hold values from -6 to 6
- obs_members: bfloat16 [128, 32, 128, 128], P('mem', 'tile'), may hold values from -38 to 38
- obs_values: float32 [32, 128, 128], P('tile', 'mem'), may hold values from -8 to 8
- obs_variance: float32 [32, 128, 128], P('tile', 'mem'), may hold values from 0.02 to 1
- obs_counts: int32 [32, 128], P('tile', 'mem'), may hold values from 0 to 128, as said below
Outputs:
- analysis: bfloat16 [128, 32, 128, 768], P('mem', 'tile')
The draws below stay inside these ranges and needn't reach their ends.
Inputs may be any that keep to these rules, and one draw needn't show every extreme that they name: obs_counts[i, j] observations of block (i, j) fill its first slots of obs_members, obs_values and obs_variance; later slots carry no observation. Some block holds 128.
All inputs are finite; a program needn't handle non-finite values.
Results may differ from the reference program's by a relative error of at most 0.012.
The reference program's roundings to bfloat16 on the way (of `scaled`, `innovation`, `mixing` and `anomaly`) count: a program that leaves them out, or rounds other values in their place, can miss the bound.
Values may be sent and summed in bfloat16 or wider, within the bound.
A program may use at most 64 MiB of HBM per device.

```python
import math
import jax
import jax.numpy as jnp
from jax import lax

MEMBERS = 128
FIELDS = 12
BLOCK = 64
CAP = 128
NS_ITERS = 12
NBR = 32
NBC = 128


def draw_obs_counts(key, part):
    key = jax.random.fold_in(key, 7)
    dense_key, sparse_key, swath_key, full_key = jax.random.split(key, 4)
    dense_counts = jax.random.randint(dense_key, (NBR, NBC), CAP // 2, CAP + 1)
    sparse_counts = jax.random.randint(sparse_key, (NBR, NBC), 0, CAP // 4 + 1)
    swath_rows = jax.random.randint(swath_key, (NBR, 1), 0, 3) == 0
    counts = jnp.where(swath_rows, dense_counts, sparse_counts)
    full_block = jax.random.randint(full_key, (), 0, NBR * NBC)
    block_ids = jnp.arange(NBR * NBC, dtype=jnp.int32).reshape(NBR, NBC)
    return jnp.where(block_ids == full_block, CAP, counts).astype(jnp.int32)


def draw_obs_members(key, part):
    key = jax.random.fold_in(key, 11)
    noise_key, member_key, slot_key = jax.random.split(key, 3)
    slot_mode = jnp.clip(jax.random.normal(slot_key, (1, NBR, NBC, CAP), jnp.float32), -3.0, 3.0)
    member_noise = jnp.clip(jax.random.normal(noise_key, (MEMBERS, NBR, NBC, CAP), jnp.float32), -6.0, 6.0)
    member_mode = jnp.clip(jax.random.normal(member_key, (MEMBERS, 1, 1, 1), jnp.float32), -3.0, 3.0)
    strength = 3.5
    return (member_noise + strength * member_mode * slot_mode).astype(jnp.bfloat16)


def block_levels(own_key, dims, cuts, low, high):
    def one(dim, shards_of):
        heights = jax.random.uniform(jax.random.fold_in(jax.random.fold_in(own_key, 6), dim), (shards_of,), jnp.float32, low / len(cuts), high / len(cuts))
        return jnp.repeat(jnp.exp(heights), dims[dim] // shards_of).reshape((-1,) + (1,) * (len(dims) - dim - 1))

    gain = one(*cuts[0])
    for cut in cuts[1:]:
        gain = gain * one(*cut)
    return gain


def bell_draw(rng, shape, scale, limit, pieces=(), kind=jnp.bfloat16):
    gain = block_levels(rng, shape, pieces, -0.22, 0.18) if pieces else 1.0
    drawn = jax.random.normal(rng, shape, jnp.float32) * scale * gain
    return jnp.minimum(jnp.maximum(drawn, -limit), limit).astype(kind)


def setup_inputs(seed: int = 0) -> dict:
    splits = jax.random.split(jax.random.key(seed), 6)
    return {
        "ensemble_state": bell_draw(splits[0], (MEMBERS, NBR, NBC, FIELDS * BLOCK), 1.0, 6.0, ((0, 32), (1, 16))),
        "obs_members": draw_obs_members(jax.random.fold_in(splits[5], 71), 0),
        "obs_values": bell_draw(splits[2], (NBR, NBC, CAP), 1.5, 8.0, ((0, 16), (1, 32)), jnp.float32),
        "obs_variance": jnp.clip(jnp.exp(math.log(1.0) - 3.912023 * jax.random.uniform(splits[3], (NBR, NBC, CAP), jnp.float32) ** block_levels(splits[3], (NBR, NBC, CAP), ((0, 16), (1, 32)), -0.2, 0.2)), 0.02, 1.0),
        "obs_counts": draw_obs_counts(jax.random.fold_in(splits[5], 71), 0),
    }


def near_sum(padded, block_rows, block_cols):
    result = None
    for row_step in range(-2, 3):
        for col_step in range(-2, 3):
            weight = math.exp(-(row_step * row_step + col_step * col_step) / 4.0)
            shifted = padded[2 + row_step:2 + row_step + block_rows, 2 + col_step:2 + col_step + block_cols]
            result = weight * shifted if result is None else result + weight * shifted
    return result

def inverse_root(system):
    count = system.shape[-1]
    scale_norm = jnp.sqrt(lax.optimization_barrier(jnp.sum(system * system, axis=(-2, -1))))
    iterate = system / scale_norm[..., None, None]
    identity = jnp.eye(count, dtype=jnp.float32)
    inverse = jnp.broadcast_to(identity, system.shape)
    for sweep_index in range(NS_ITERS):
        factor = 1.5 * identity - 0.5 * jnp.matmul(inverse, iterate, precision=lax.Precision.HIGHEST)
        iterate = jnp.matmul(iterate, factor, precision=lax.Precision.HIGHEST)
        inverse = jnp.matmul(factor, inverse, precision=lax.Precision.HIGHEST)
    return inverse / jnp.sqrt(scale_norm)[..., None, None]

def reference(ensemble_state, obs_members, obs_values, obs_variance, obs_counts):
    member_values = obs_members.astype(jnp.float32)
    obs_mean = lax.optimization_barrier(jnp.sum(member_values, axis=0)) / MEMBERS
    slot_index = jnp.arange(CAP, dtype=jnp.int32)
    usable = slot_index[None, None, :] < obs_counts[:, :, None]
    root_weight = jnp.where(usable, 1.0 / jnp.sqrt(obs_variance), jnp.float32(0.0))
    scaled = ((member_values - obs_mean) * root_weight).astype(jnp.bfloat16)
    innovation = (root_weight * (obs_values - obs_mean)).astype(jnp.bfloat16)
    scaled_wide = scaled.astype(jnp.float32)
    gram_blocks = jnp.einsum('kijc,lijc->ijkl', scaled_wide, scaled_wide)
    drive_terms = jnp.einsum('kijc,ijc->ijk', scaled_wide, innovation.astype(jnp.float32))
    gram_padded = jnp.pad(gram_blocks, ((2, 2), (2, 2), (0, 0), (0, 0)))
    drive_padded = jnp.pad(drive_terms, ((2, 2), (2, 2), (0, 0)))
    total_gram = near_sum(gram_padded, NBR, NBC)
    total_drive = near_sum(drive_padded, NBR, NBC)
    system = total_gram + (MEMBERS - 1) * jnp.eye(MEMBERS, dtype=jnp.float32)
    inverse = inverse_root(system)
    inner = jnp.einsum('ijkl,ijl->ijk', inverse, total_drive, precision=lax.Precision.HIGHEST)
    mean_weight = jnp.einsum('ijkl,ijl->ijk', inverse, inner, precision=lax.Precision.HIGHEST)
    mixing = (math.sqrt(MEMBERS - 1) * inverse + mean_weight[..., :, None]).astype(jnp.bfloat16)
    state_values = ensemble_state.astype(jnp.float32)
    state_mean = lax.optimization_barrier(jnp.sum(state_values, axis=0)) / MEMBERS
    anomaly = (state_values - state_mean).astype(jnp.bfloat16)

    def row_analysis(operands):
        anomaly_row, mixing_row, mean_row = operands
        update = jnp.einsum('kjf,jkl->ljf', anomaly_row.astype(jnp.float32), mixing_row.astype(jnp.float32))
        return (mean_row + update).astype(jnp.bfloat16)
    stacked = lax.map(row_analysis, (jnp.moveaxis(anomaly, 1, 0), mixing, state_mean))
    return jnp.moveaxis(stacked, 0, 1)
```

```python
import functools
import math

import jax
import jax.numpy as jnp
from jax import lax
from jax.experimental import pallas as pl
from jax.experimental.pallas import tpu as pltpu
from jax.sharding import PartitionSpec as P

NS_ITERS = 12
MESH = pl.DeviceIdType.MESH
BF = jnp.bfloat16
F32 = jnp.float32
W1 = math.exp(-0.25)
W2 = math.exp(-1.0)
NEAR = (W2, W1, 1.0, W1, W2)
K = 128
EXT = 144
ROWS = 136


def iota(shape, dim):
    return lax.broadcasted_iota(jnp.int32, shape, dim)


def dot(a, b):
    return lax.dot_general(a, b, (((1,), (0,)), ((), ())), preferred_element_type=F32)


def dot_t(a, b):
    return lax.dot_general(a, b, (((1,), (1,)), ((), ())), preferred_element_type=F32)


def one_hot(hit):
    return jnp.where(hit, 1.0, 0.0).astype(BF)


def split2(value):
    high = value.astype(BF)
    return high, (value - high.astype(F32)).astype(BF)


def split3(value):
    high = value.astype(BF)
    rest = value - high.astype(F32)
    mid = rest.astype(BF)
    return high, mid, (rest - mid.astype(F32)).astype(BF)


def right2(high, low):
    pair = jnp.concatenate([high, low], axis=1)
    return jnp.concatenate([pair, pair], axis=0)


def mul2(left, right):
    both = dot(jnp.concatenate(split2(left), axis=1), right)
    return both[:, :K] + both[:, K:]


def right3(parts):
    high, mid, low = parts
    return right2(high, mid), jnp.concatenate([high, low], axis=0)


def mul3(left, right):
    high, mid, low = split3(left)
    both = dot(jnp.concatenate([high, mid], axis=1), right[0])
    small = dot(jnp.concatenate([low, high], axis=1), right[1])
    return both[:, :K] + (both[:, K:] + small)


def kernel(
    state, obs, values, variance, counts, out,
    obs_out, obs_in, state_out, state_in, res_out, res_in,
    scaled, grams, sums, above, below, root, inv, mix, perm, perm_back,
    obs_s, obs_r, state_s, state_r, col_s, col_r, row_s, row_r, res_s, res_r,
):
    mem, tile = lax.axis_index("mem"), lax.axis_index("tile")
    mems, tiles = 32, 16
    z, y, x = mem // 16, lax.rem(mem // 4, 4), lax.rem(mem, 4)

    def partner(step):
        pz = lax.rem(z + step // 16, 2)
        py = lax.rem(y + lax.rem(step // 4, 4), 4)
        px = lax.rem(x + lax.rem(step, 4), 4)
        return pz * 16 + py * 4 + px

    barrier = pltpu.get_barrier_semaphore()

    @pl.loop(1, mems)
    def _(step):
        pl.semaphore_signal(barrier, inc=1, device_id={"mem": partner(step)}, device_id_type=MESH)

    @pl.when(tile > 0)
    def _():
        pl.semaphore_signal(barrier, inc=1, device_id={"tile": tile - 1}, device_id_type=MESH)

    @pl.when(tile < tiles - 1)
    def _():
        pl.semaphore_signal(barrier, inc=1, device_id={"tile": tile + 1}, device_id_type=MESH)

    r, c = iota((64, 64), 0), iota((64, 64), 1)
    pack = one_hot(c == (r % 4) * 16 + (r // 16) * 4 + (r // 4) % 4)
    unpack = one_hot(r == (c % 4) * 16 + (c // 16) * 4 + (c // 4) % 4)

    def packed(source, target):
        for i in range(2):
            for q in range(8):
                rows = jnp.concatenate([source[k, i, 16 * q:16 * q + 16, :] for k in range(4)], axis=0)
                moved = dot(pack, rows).astype(BF)
                for d in range(4):
                    target[4 * q + d, i] = moved[16 * d:16 * d + 16]

    packed(obs, obs_out)
    obs_in[mem] = obs_out[mem]

    @pl.when(tile == 0)
    def _():
        pl.semaphore_wait(barrier, mems)

    @pl.when(tile == tiles - 1)
    def _():
        pl.semaphore_wait(barrier, mems)

    @pl.when(jnp.logical_and(tile > 0, tile < tiles - 1))
    def _():
        pl.semaphore_wait(barrier, mems + 1)

    def send_all(source, target, send, receive, first, last):
        @pl.loop(first, last)
        def _(step):
            to = partner(step)
            pltpu.make_async_remote_copy(
                src_ref=source.at[to], dst_ref=target.at[mem], send_sem=send, recv_sem=receive,
                device_id={"mem": to}, device_id_type=MESH,
            ).start()

    def take(ref, semaphore):
        pltpu.make_async_copy(ref, ref, semaphore).wait()

    send_all(obs_out, obs_in, obs_s, obs_r, 16, 32)
    send_all(obs_out, obs_in, obs_s, obs_r, 1, 16)

    packed(state, state_out)
    state_in[mem] = state_out[mem]
    r, c = iota((512, 512), 0), iota((512, 512), 1)
    perm[...] = one_hot(c == ((r // 4) % 32) * 16 + (r // 128) * 4 + r % 4)
    perm_back[...] = one_hot(r == ((c // 4) % 32) * 16 + (c // 128) * 4 + c % 4)

    some = pl.ds(0, mems - 1)
    take(obs_out.at[some], obs_s)
    send_all(state_out, state_in, state_s, state_r, 16, 32)
    take(obs_in.at[some], obs_r)

    slot = iota((1, 128), 1)
    for i in range(2):
        wide = dot(perm[...], obs_in[:, i].reshape(512, 128))
        for j in range(4):
            member = wide[128 * j:128 * j + 128]
            mean = jnp.sum(member, axis=0, keepdims=True) * (1.0 / K)
            weight = jnp.where(slot < counts[i, j], 1.0 / jnp.sqrt(variance[i, j:j + 1, :]), 0.0)
            innovation = weight * (values[i, j:j + 1, :] - mean)
            scaled[j + 2, i, 0:K] = ((member - mean) * weight).astype(BF)
            scaled[j + 2, i, K:EXT] = jnp.where(
                iota((16, 128), 0) == 0, jnp.broadcast_to(innovation, (16, 128)), 0.0
            ).astype(BF)

    def to_left():
        return pltpu.make_async_remote_copy(
            src_ref=scaled.at[pl.ds(2, 2)], dst_ref=scaled.at[pl.ds(6, 2)], send_sem=col_s.at[0],
            recv_sem=col_r.at[0], device_id={"mem": mem - 1}, device_id_type=MESH)

    def to_right():
        return pltpu.make_async_remote_copy(
            src_ref=scaled.at[pl.ds(4, 2)], dst_ref=scaled.at[pl.ds(0, 2)], send_sem=col_s.at[1],
            recv_sem=col_r.at[1], device_id={"mem": mem + 1}, device_id_type=MESH)

    @pl.when(mem > 0)
    def _():
        to_left().start()

    @pl.when(mem < mems - 1)
    def _():
        to_right().start()

    @pl.when(mem == 0)
    def _():
        scaled[0:2] = jnp.zeros((2, 2, EXT, 128), BF)

    @pl.when(mem == mems - 1)
    def _():
        scaled[6:8] = jnp.zeros((2, 2, EXT, 128), BF)

    def gram(col):
        for i in range(2):
            grams[col, i] = dot_t(scaled[col, i], scaled[col, i, 0:K])[:ROWS]

    for col in range(2, 6):
        gram(col)

    @pl.when(mem > 0)
    def _():
        to_left().wait_send()
        to_right().wait_recv()

    @pl.when(mem < mems - 1)
    def _():
        to_right().wait_send()
        to_left().wait_recv()

    for col in (0, 1, 6, 7):
        gram(col)
    for i in range(2):
        for j in range(4):
            total = NEAR[0] * grams[j, i]
            for b in range(1, 5):
                total = total + NEAR[b] * grams[j + b, i]
            sums[i, j] = total

    def to_above():
        return pltpu.make_async_remote_copy(
            src_ref=sums, dst_ref=below, send_sem=row_s.at[0], recv_sem=row_r.at[0],
            device_id={"tile": tile - 1}, device_id_type=MESH)

    def to_below():
        return pltpu.make_async_remote_copy(
            src_ref=sums, dst_ref=above, send_sem=row_s.at[1], recv_sem=row_r.at[1],
            device_id={"tile": tile + 1}, device_id_type=MESH)

    @pl.when(tile > 0)
    def _():
        to_above().start()

    @pl.when(tile < tiles - 1)
    def _():
        to_below().start()

    @pl.when(tile == 0)
    def _():
        above[...] = jnp.zeros(above.shape, F32)

    @pl.when(tile == tiles - 1)
    def _():
        below[...] = jnp.zeros(below.shape, F32)

    @pl.when(tile > 0)
    def _():
        to_above().wait_send()
        to_below().wait_recv()

    @pl.when(tile < tiles - 1)
    def _():
        to_below().wait_send()
        to_above().wait_recv()

    send_all(state_out, state_in, state_s, state_r, 1, 16)

    eye = jnp.where(iota((K, K), 0) == iota((K, K), 1), 1.0, 0.0).astype(F32)
    drives, norms = [], []
    for i in range(2):
        for j in range(4):
            b = 4 * i + j
            if i == 0:
                total = sums[0, j] + W1 * sums[1, j] + (W2 * above[0, j] + W1 * above[1, j]) + W2 * below[0, j]
            else:
                total = sums[1, j] + W1 * sums[0, j] + W2 * above[1, j] + (W1 * below[0, j] + W2 * below[1, j])
            system = total[:K] + (K - 1) * eye
            norm = jnp.sqrt(jnp.sum(jnp.sum(system * system, axis=1, keepdims=True), axis=0, keepdims=True))
            drives.append(total[K:ROWS])
            norms.append(norm)
            first = system / norm
            factor = 1.5 * eye - 0.5 * first
            right = right3(split3(factor))
            root[b] = mul3(mul3(first, right), right)
            inv[b] = factor

    for b in range(8):
        factor = 1.5 * eye - 0.5 * root[b]
        right = right3(split3(factor))
        inv[b] = mul3(inv[b], right)
        root[b] = mul3(mul3(root[b], right), right)

    @pl.loop(2, NS_ITERS - 1)
    def _(sweep):
        for b in range(8):
            factor = 1.5 * eye - 0.5 * root[b]
            right = right2(*split2(factor))
            inv[b] = mul2(inv[b], right)
            root[b] = mul2(mul2(root[b], right), right)

    for b in range(8):
        factor = 1.5 * eye - 0.5 * root[b]
        inverse = mul2(inv[b], right2(*split2(factor))) / jnp.sqrt(norms[b])
        right = right2(*split2(inverse))
        shift = mul2(mul2(drives[b], right), right)[0:1]
        mix[b] = (math.sqrt(K - 1) * inverse + shift).astype(BF)

    take(state_out.at[some], state_s)
    take(state_in.at[some], state_r)

    def send_result(i, first, last):
        send_all(res_out.at[i], res_in.at[i], res_s.at[i], res_r.at[i], first, last)

    for i in range(2):
        wide = dot(perm[...], state_in[:, i].reshape(512, 768))
        rows = []
        for j in range(4):
            member = wide[128 * j:128 * j + 128]
            mean = jnp.sum(member, axis=0, keepdims=True) * (1.0 / K)
            rows.append((mean + dot(mix[4 * i + j], (member - mean).astype(BF))).astype(BF))
        moved = dot(perm_back[...], jnp.concatenate(rows, axis=0)).astype(BF)
        res_out[i] = moved.reshape(32, 16, 768)
        send_result(i, 16, 32)
        send_result(i, 1, 16)
        res_in[i, mem] = res_out[i, mem]

    for i in range(2):
        take(res_in.at[i, some], res_r.at[i])
        for q in range(8):
            moved = dot(unpack, res_in[i, 4 * q:4 * q + 4].reshape(64, 768)).astype(BF)
            for k in range(4):
                out[k, i, 16 * q:16 * q + 16, :] = moved[16 * k:16 * k + 16]
        take(res_out.at[i, some], res_s.at[i])


def on_device(ensemble_state, obs_members, obs_values, obs_variance, obs_counts):
    vmem = pl.BlockSpec(memory_space=pltpu.VMEM)
    dma, dmas = pltpu.SemaphoreType.DMA(()), pltpu.SemaphoreType.DMA((2,))
    obs_box, state_box = pltpu.VMEM((32, 2, 16, 128), BF), pltpu.VMEM((32, 2, 16, 768), BF)
    res_box = pltpu.VMEM((2, 32, 16, 768), BF)
    sum_box = pltpu.VMEM((2, 4, ROWS, 128), F32)
    square = pltpu.VMEM((8, K, K), F32)
    return pl.pallas_call(
        kernel,
        out_shape=jax.ShapeDtypeStruct(ensemble_state.shape, BF),
        in_specs=[vmem, vmem, vmem, vmem, pl.BlockSpec(memory_space=pltpu.SMEM)],
        out_specs=vmem,
        scratch_shapes=[
            obs_box, obs_box, state_box, state_box, res_box, res_box,
            pltpu.VMEM((8, 2, EXT, 128), BF), pltpu.VMEM((8, 2, ROWS, 128), F32),
            sum_box, sum_box, sum_box, square, square, pltpu.VMEM((8, K, K), BF),
            pltpu.VMEM((512, 512), BF), pltpu.VMEM((512, 512), BF),
            dma, dma, dma, dma, dmas, dmas, dmas, dmas, dmas, dmas,
        ],
        compiler_params=pltpu.CompilerParams(
            collective_id=0, has_side_effects=True, vmem_limit_bytes=48 * 1024 * 1024
        ),
        cost_estimate=pl.CostEstimate(flops=10**10, bytes_accessed=4 * 10**6, transcendentals=0),
        name="letkf",
    )(ensemble_state, obs_members, obs_values, obs_variance, obs_counts)


def solution(mesh):
    placed = (
        P("mem", "tile", None, None),
        P("mem", "tile", None, None),
        P("tile", "mem", None),
        P("tile", "mem", None),
        P("tile", "mem"),
    )
    return jax.shard_map(
        on_device,
        mesh=mesh,
        in_specs=placed,
        out_specs=P("mem", "tile", None, None),
        check_vma=False,
    )
```

```python
import functools
import math

import jax
import jax.numpy as jnp
from jax import lax
from jax.experimental import pallas as pl
from jax.experimental.pallas import tpu as pltpu
from jax.sharding import PartitionSpec as P

NS_ITERS = 12
MESH = pl.DeviceIdType.MESH
BF = jnp.bfloat16
F32 = jnp.float32
W1 = math.exp(-0.25)
W2 = math.exp(-1.0)
NEAR = (W2, W1, 1.0, W1, W2)
K = 128
EXT = 144
ROWS = 136
FIRST = 2


def iota(shape, dim):
    return lax.broadcasted_iota(jnp.int32, shape, dim)


def dot(a, b):
    return lax.dot_general(a, b, (((1,), (0,)), ((), ())), preferred_element_type=F32)


def dot_t(a, b):
    return lax.dot_general(a, b, (((1,), (1,)), ((), ())), preferred_element_type=F32)


def one_hot(hit):
    return jnp.where(hit, 1.0, 0.0).astype(BF)


def split2(value):
    high = value.astype(BF)
    return high, (value - high.astype(F32)).astype(BF)


def split3(value):
    high = value.astype(BF)
    rest = value - high.astype(F32)
    mid = rest.astype(BF)
    return high, mid, (rest - mid.astype(F32)).astype(BF)


def right2(high, low):
    pair = jnp.concatenate([high, low], axis=1)
    return jnp.concatenate([pair, pair], axis=0)


def mul2(left, right):
    both = dot(jnp.concatenate(split2(left), axis=1), right)
    return both[:, :K] + both[:, K:]


def right3(parts):
    high, mid, low = parts
    return right2(high, mid), jnp.concatenate([high, low], axis=0)


def mul3(left, right):
    high, mid, low = split3(left)
    both = dot(jnp.concatenate([high, mid], axis=1), right[0])
    small = dot(jnp.concatenate([low, high], axis=1), right[1])
    return both[:, :K] + (both[:, K:] + small)


def kernel(
    state_hbm, obs_hbm, values_hbm, variance_hbm, counts_hbm, out_hbm,
    state, obs, values, variance, counts, out,
    obs_out, obs_in, state_out, state_in, res_out, res_in,
    far_out, far_in, weights, far_weights, scaled, grams, sums, above, below, root, inv, mix, perm, perm_back,
    load_s, store_s, far_s, far_r, weight_s, weight_r,
    obs_s, obs_r, state_s, state_r, col_s, col_r, row_s, row_r, res_s, res_r,
):
    mem, tile = lax.axis_index("mem"), lax.axis_index("tile")
    mems, tiles, middle = 32, 16, 15
    z, y, x = mem // 16, lax.rem(mem // 4, 4), lax.rem(mem, 4)

    def partner(step):
        pz = lax.rem(z + step // 16, 2)
        py = lax.rem(y + lax.rem(step // 4, 4), 4)
        px = lax.rem(x + lax.rem(step, 4), 4)
        return pz * 16 + py * 4 + px

    loads = [
        pltpu.make_async_copy(source, target, load_s.at[n]) for n, (source, target) in enumerate((
            (obs_hbm, obs), (values_hbm, values), (variance_hbm, variance), (counts_hbm, counts),
            (state_hbm, state)))
    ]
    for load in loads:
        load.start()
    barrier = pltpu.get_barrier_semaphore()

    @pl.loop(1, mems)
    def _(step):
        pl.semaphore_signal(barrier, inc=1, device_id={"mem": partner(step)}, device_id_type=MESH)

    @pl.when(tile > 0)
    def _():
        pl.semaphore_signal(barrier, inc=1, device_id={"tile": tile - 1}, device_id_type=MESH)

    @pl.when(tile < tiles - 1)
    def _():
        pl.semaphore_signal(barrier, inc=1, device_id={"tile": tile + 1}, device_id_type=MESH)

    r, c = iota((64, 64), 0), iota((64, 64), 1)
    pack = one_hot(c == (r % 4) * 16 + (r // 16) * 4 + (r // 4) % 4)
    unpack = one_hot(r == (c % 4) * 16 + (c // 16) * 4 + (c // 4) % 4)

    def packed(source, target, far=None):
        edges = ([], [])
        for i in range(2):
            for q in range(8):
                rows = jnp.concatenate([source[k, i, 16 * q:16 * q + 16, :] for k in range(4)], axis=0)
                wide = dot(pack, rows)
                moved = wide.astype(BF)
                for d in range(4):
                    target[4 * q + d, i] = moved[16 * d:16 * d + 16]
                if far is not None and q == 4:
                    edges[0].append(wide[0:8])
                if far is not None and q == 3:
                    edges[1].append(wide[56:64])
        if far is not None:
            for side in range(2):
                far[side] = jnp.concatenate(edges[side], axis=0).astype(BF)

    loads[0].wait()
    packed(obs, obs_out, far_out)
    obs_in[mem] = obs_out[mem]
    for load in loads[1:4]:
        load.wait()
    slot = iota((1, 128), 1)
    for i in range(2):
        for j in range(4):
            b = 4 * i + j
            weights[0, b:b + 1] = jnp.where(
                slot < counts[i, j], 1.0 / jnp.sqrt(variance[i, j:j + 1, :]), 0.0)
            weights[1, b:b + 1] = values[i, j:j + 1, :]

    @pl.when(tile == 0)
    def _():
        pl.semaphore_wait(barrier, mems)

    @pl.when(tile == tiles - 1)
    def _():
        pl.semaphore_wait(barrier, mems)

    @pl.when(jnp.logical_and(tile > 0, tile < tiles - 1))
    def _():
        pl.semaphore_wait(barrier, mems + 1)

    def send_all(source, target, send, receive, first, last):
        @pl.loop(first, last)
        def _(step):
            to = partner(step)
            pltpu.make_async_remote_copy(
                src_ref=source.at[to], dst_ref=target.at[mem], send_sem=send, recv_sem=receive,
                device_id={"mem": to}, device_id_type=MESH,
            ).start()

    def take(ref, semaphore):
        pltpu.make_async_copy(ref, ref, semaphore).wait()

    send_all(obs_out, obs_in, obs_s, obs_r, 16, 32)
    send_all(obs_out, obs_in, obs_s, obs_r, 1, 16)

    def to_middle(side):
        return pltpu.make_async_remote_copy(
            src_ref=far_out.at[side], dst_ref=far_in.at[mem], send_sem=far_s.at[side], recv_sem=far_r,
            device_id={"mem": middle + side}, device_id_type=MESH)

    def weights_over(side):
        return pltpu.make_async_remote_copy(
            src_ref=weights, dst_ref=far_weights, send_sem=weight_s, recv_sem=weight_r,
            device_id={"mem": middle + 1 - side}, device_id_type=MESH)

    for side in range(2):
        @pl.when(mem != middle + side)
        def _(side=side):
            to_middle(side).start()

        @pl.when(mem == middle + side)
        def _(side=side):
            weights_over(side).start()
            far_in[mem] = far_out[side]

    loads[4].wait()
    packed(state, state_out)
    state_in[mem] = state_out[mem]
    r, c = iota((512, 512), 0), iota((512, 512), 1)
    perm[...] = one_hot(c == ((r // 4) % 32) * 16 + (r // 128) * 4 + r % 4)
    perm_back[...] = one_hot(r == ((c // 4) % 32) * 16 + (c // 128) * 4 + c % 4)

    some = pl.ds(0, mems - 1)
    take(obs_out.at[some], obs_s)
    send_all(state_out, state_in, state_s, state_r, 16, 16 + FIRST)
    take(obs_in.at[some], obs_r)

    def scale(member, given, b, col, i):
        mean = jnp.sum(member, axis=0, keepdims=True) * (1.0 / K)
        weight = given[0, b:b + 1]
        innovation = weight * (given[1, b:b + 1] - mean)
        scaled[col, i, 0:K] = ((member - mean) * weight).astype(BF)
        scaled[col, i, K:EXT] = jnp.where(
            iota((16, 128), 0) == 0, jnp.broadcast_to(innovation, (16, 128)), 0.0
        ).astype(BF)

    for i in range(2):
        wide = dot(perm[...], obs_in[:, i].reshape(512, 128))
        for j in range(4):
            scale(wide[128 * j:128 * j + 128], weights, 4 * i + j, j + 2, i)

    def to_left():
        return pltpu.make_async_remote_copy(
            src_ref=scaled.at[pl.ds(2, 2)], dst_ref=scaled.at[pl.ds(6, 2)], send_sem=col_s.at[0],
            recv_sem=col_r.at[0], device_id={"mem": mem - 1}, device_id_type=MESH)

    def to_right():
        return pltpu.make_async_remote_copy(
            src_ref=scaled.at[pl.ds(4, 2)], dst_ref=scaled.at[pl.ds(0, 2)], send_sem=col_s.at[1],
            recv_sem=col_r.at[1], device_id={"mem": mem + 1}, device_id_type=MESH)

    has_left = jnp.logical_and(mem != 0, mem != middle + 1)
    has_right = jnp.logical_and(mem != mems - 1, mem != middle)

    @pl.when(has_left)
    def _():
        to_left().start()

    @pl.when(has_right)
    def _():
        to_right().start()

    for side in range(2):
        @pl.when(mem == middle + side)
        def _(side=side):
            take(far_in.at[some], far_r)
            weights_over(side).wait()
            wide = dot(perm[...], far_in[...].reshape(512, 128))
            for i in range(2):
                for jj in range(2):
                    n = 2 * i + jj
                    scale(wide[128 * n:128 * n + 128], far_weights, 4 * i + 2 * side + jj, 6 - 6 * side + jj, i)

        @pl.when(mem != middle + side)
        def _(side=side):
            to_middle(side).wait_send()

    @pl.when(mem == 0)
    def _():
        scaled[0:2] = jnp.zeros((2, 2, EXT, 128), BF)

    @pl.when(mem == mems - 1)
    def _():
        scaled[6:8] = jnp.zeros((2, 2, EXT, 128), BF)

    def gram(col):
        for i in range(2):
            grams[col, i] = dot_t(scaled[col, i], scaled[col, i, 0:K])[:ROWS]

    for col in range(2, 6):
        gram(col)

    @pl.when(has_left)
    def _():
        to_left().wait_send()
        to_right().wait_recv()

    @pl.when(has_right)
    def _():
        to_right().wait_send()
        to_left().wait_recv()

    for col in (0, 1, 6, 7):
        gram(col)
    for i in range(2):
        for j in range(4):
            total = NEAR[0] * grams[j, i]
            for b in range(1, 5):
                total = total + NEAR[b] * grams[j + b, i]
            sums[i, j] = total

    def to_above():
        return pltpu.make_async_remote_copy(
            src_ref=sums, dst_ref=below, send_sem=row_s.at[0], recv_sem=row_r.at[0],
            device_id={"tile": tile - 1}, device_id_type=MESH)

    def to_below():
        return pltpu.make_async_remote_copy(
            src_ref=sums, dst_ref=above, send_sem=row_s.at[1], recv_sem=row_r.at[1],
            device_id={"tile": tile + 1}, device_id_type=MESH)

    @pl.when(tile > 0)
    def _():
        to_above().start()

    @pl.when(tile < tiles - 1)
    def _():
        to_below().start()

    @pl.when(tile == 0)
    def _():
        above[...] = jnp.zeros(above.shape, F32)

    @pl.when(tile == tiles - 1)
    def _():
        below[...] = jnp.zeros(below.shape, F32)

    @pl.when(tile > 0)
    def _():
        to_above().wait_send()
        to_below().wait_recv()

    @pl.when(tile < tiles - 1)
    def _():
        to_below().wait_send()
        to_above().wait_recv()

    send_all(state_out, state_in, state_s, state_r, 16 + FIRST, 32)
    send_all(state_out, state_in, state_s, state_r, 1, 16)

    eye = jnp.where(iota((K, K), 0) == iota((K, K), 1), 1.0, 0.0).astype(F32)
    drives, norms = [], []
    for i in range(2):
        for j in range(4):
            b = 4 * i + j
            if i == 0:
                total = sums[0, j] + W1 * sums[1, j] + (W2 * above[0, j] + W1 * above[1, j]) + W2 * below[0, j]
            else:
                total = sums[1, j] + W1 * sums[0, j] + W2 * above[1, j] + (W1 * below[0, j] + W2 * below[1, j])
            system = total[:K] + (K - 1) * eye
            norm = jnp.sqrt(jnp.sum(jnp.sum(system * system, axis=1, keepdims=True), axis=0, keepdims=True))
            drives.append(total[K:ROWS])
            norms.append(norm)
            first = system / norm
            factor = 1.5 * eye - 0.5 * first
            right = right3(split3(factor))
            root[b] = mul3(mul3(first, right), right)
            inv[b] = factor

    for b in range(8):
        factor = 1.5 * eye - 0.5 * root[b]
        right = right3(split3(factor))
        inv[b] = mul3(inv[b], right)
        root[b] = mul3(mul3(root[b], right), right)

    @pl.loop(2, NS_ITERS - 1)
    def _(sweep):
        for b in range(8):
            factor = 1.5 * eye - 0.5 * root[b]
            right = right2(*split2(factor))
            inv[b] = mul2(inv[b], right)
            root[b] = mul2(mul2(root[b], right), right)

    for b in range(8):
        factor = 1.5 * eye - 0.5 * root[b]
        inverse = mul2(inv[b], right2(*split2(factor))) / jnp.sqrt(norms[b])
        right = right2(*split2(inverse))
        shift = mul2(mul2(drives[b], right), right)[0:1]
        mix[b] = (math.sqrt(K - 1) * inverse + shift).astype(BF)

    take(state_out.at[some], state_s)
    take(state_in.at[some], state_r)

    def send_result(i, first, last):
        send_all(res_out.at[i], res_in.at[i], res_s.at[i], res_r.at[i], first, last)

    for i in range(2):
        wide = dot(perm[...], state_in[:, i].reshape(512, 768))
        rows = []
        for j in range(4):
            member = wide[128 * j:128 * j + 128]
            mean = jnp.sum(member, axis=0, keepdims=True) * (1.0 / K)
            rows.append((mean + dot(mix[4 * i + j], (member - mean).astype(BF))).astype(BF))
        moved = dot(perm_back[...], jnp.concatenate(rows, axis=0)).astype(BF)
        res_out[i] = moved.reshape(32, 16, 768)
        send_result(i, 16, 32)
        send_result(i, 1, 16)
        res_in[i, mem] = res_out[i, mem]

    for i in range(2):
        take(res_in.at[i, some], res_r.at[i])
        for q in range(8):
            moved = dot(unpack, res_in[i, 4 * q:4 * q + 4].reshape(64, 768)).astype(BF)
            for k in range(4):
                out[i, k, 16 * q:16 * q + 16, :] = moved[16 * k:16 * k + 16]
        for k in range(4):
            pltpu.make_async_copy(out.at[i, k], out_hbm.at[k, i], store_s.at[i, k]).start()
        take(res_out.at[i, some], res_s.at[i])
    for i in range(2):
        for k in range(4):
            pltpu.make_async_copy(out.at[i, k], out_hbm.at[k, i], store_s.at[i, k]).wait()


def on_device(ensemble_state, obs_members, obs_values, obs_variance, obs_counts):
    hbm = pl.BlockSpec(memory_space=pl.ANY)
    dma, dmas = pltpu.SemaphoreType.DMA(()), pltpu.SemaphoreType.DMA((2,))
    obs_box, state_box = pltpu.VMEM((32, 2, 16, 128), BF), pltpu.VMEM((32, 2, 16, 768), BF)
    res_box = pltpu.VMEM((2, 32, 16, 768), BF)
    sum_box = pltpu.VMEM((2, 4, ROWS, 128), F32)
    square = pltpu.VMEM((8, K, K), F32)
    return pl.pallas_call(
        kernel,
        out_shape=jax.ShapeDtypeStruct(ensemble_state.shape, BF),
        in_specs=[hbm] * 5,
        out_specs=hbm,
        scratch_shapes=[
            pltpu.VMEM((4, 2, 128, 768), BF), pltpu.VMEM((4, 2, 128, 128), BF), pltpu.VMEM((2, 4, 128), F32),
            pltpu.VMEM((2, 4, 128), F32), pltpu.SMEM((2, 4), jnp.int32), pltpu.VMEM((2, 4, 128, 768), BF),
            obs_box, obs_box, state_box, state_box, res_box, res_box,
            pltpu.VMEM((2, 16, 128), BF), pltpu.VMEM((32, 16, 128), BF),
            pltpu.VMEM((2, 8, 128), F32), pltpu.VMEM((2, 8, 128), F32),
            pltpu.VMEM((8, 2, EXT, 128), BF), pltpu.VMEM((8, 2, ROWS, 128), F32),
            sum_box, sum_box, sum_box, square, square, pltpu.VMEM((8, K, K), BF),
            pltpu.VMEM((512, 512), BF), pltpu.VMEM((512, 512), BF),
            pltpu.SemaphoreType.DMA((5,)), pltpu.SemaphoreType.DMA((2, 4)), dmas, dma, dma, dma,
            dma, dma, dma, dma, dmas, dmas, dmas, dmas, dmas, dmas,
        ],
        compiler_params=pltpu.CompilerParams(
            collective_id=0, has_side_effects=True, vmem_limit_bytes=64 * 1024 * 1024
        ),
        cost_estimate=pl.CostEstimate(flops=10**10, bytes_accessed=4 * 10**6, transcendentals=0),
        name="letkf",
    )(ensemble_state, obs_members, obs_values, obs_variance, obs_counts)


def solution(mesh):
    placed = (
        P("mem", "tile", None, None),
        P("mem", "tile", None, None),
        P("tile", "mem", None),
        P("tile", "mem", None),
        P("tile", "mem"),
    )
    return jax.shard_map(
        on_device,
        mesh=mesh,
        in_specs=placed,
        out_specs=P("mem", "tile", None, None),
        check_vma=False,
    )
```

```python
import functools
import math

import jax
import jax.numpy as jnp
from jax import lax
from jax.experimental import pallas as pl
from jax.experimental.pallas import tpu as pltpu
from jax.sharding import PartitionSpec as P

NS_ITERS = 12
MESH = pl.DeviceIdType.MESH
BF = jnp.bfloat16
F32 = jnp.float32
W1 = math.exp(-0.25)
W2 = math.exp(-1.0)
NEAR = (W2, W1, 1.0, W1, W2)
K = 128
EXT = 144
ROWS = 136
FIRST = 4


def iota(shape, dim):
    return lax.broadcasted_iota(jnp.int32, shape, dim)


def dot(a, b):
    return lax.dot_general(a, b, (((1,), (0,)), ((), ())), preferred_element_type=F32)


def dot_t(a, b):
    return lax.dot_general(a, b, (((1,), (1,)), ((), ())), preferred_element_type=F32)


def one_hot(hit):
    return jnp.where(hit, 1.0, 0.0).astype(BF)


def split2(value):
    high = value.astype(BF)
    return high, (value - high.astype(F32)).astype(BF)


def split3(value):
    high = value.astype(BF)
    rest = value - high.astype(F32)
    mid = rest.astype(BF)
    return high, mid, (rest - mid.astype(F32)).astype(BF)


def right2(high, low):
    pair = jnp.concatenate([high, low], axis=1)
    return jnp.concatenate([pair, pair], axis=0)


def mul2(left, right):
    both = dot(jnp.concatenate(split2(left), axis=1), right)
    return both[:, :K] + both[:, K:]


def right3(parts):
    high, mid, low = parts
    return right2(high, mid), jnp.concatenate([high, low], axis=0)


def mul3(left, right):
    high, mid, low = split3(left)
    both = dot(jnp.concatenate([high, mid], axis=1), right[0])
    small = dot(jnp.concatenate([low, high], axis=1), right[1])
    return both[:, :K] + (both[:, K:] + small)


def kernel(
    state_hbm, obs_hbm, values_hbm, variance_hbm, counts_hbm, out_hbm,
    state, obs, values, variance, counts, out,
    obs_out, obs_in, state_out, state_in, res_out, res_in,
    far_out, far_in, weights, far_weights, scaled, grams, sums, above, below, root, inv, mix, perm, perm_back,
    load_s, store_s, far_s, far_r, weight_s, weight_r,
    obs_s, obs_r, state_s, state_r, col_s, col_r, row_s, row_r, res_s, res_r,
):
    mem, tile = lax.axis_index("mem"), lax.axis_index("tile")
    mems, tiles, middle = 32, 16, 15
    z, y, x = mem // 16, lax.rem(mem // 4, 4), lax.rem(mem, 4)

    def partner(step):
        pz = lax.rem(z + step // 16, 2)
        py = lax.rem(y + lax.rem(step // 4, 4), 4)
        px = lax.rem(x + lax.rem(step, 4), 4)
        return pz * 16 + py * 4 + px

    loads = [
        pltpu.make_async_copy(source, target, load_s.at[n]) for n, (source, target) in enumerate((
            (obs_hbm, obs), (values_hbm, values), (variance_hbm, variance), (counts_hbm, counts),
            (state_hbm, state)))
    ]
    for load in loads:
        load.start()
    barrier = pltpu.get_barrier_semaphore()

    @pl.loop(1, mems)
    def _(step):
        pl.semaphore_signal(barrier, inc=1, device_id={"mem": partner(step)}, device_id_type=MESH)

    @pl.when(tile > 0)
    def _():
        pl.semaphore_signal(barrier, inc=1, device_id={"tile": tile - 1}, device_id_type=MESH)

    @pl.when(tile < tiles - 1)
    def _():
        pl.semaphore_signal(barrier, inc=1, device_id={"tile": tile + 1}, device_id_type=MESH)

    r, c = iota((64, 64), 0), iota((64, 64), 1)
    pack = one_hot(c == (r % 4) * 16 + (r // 16) * 4 + (r // 4) % 4)
    unpack = one_hot(r == (c % 4) * 16 + (c // 16) * 4 + (c // 4) % 4)

    def packed(source, target, place, far=None):
        edges = ([], [])
        for i in range(2):
            for q in range(8):
                rows = jnp.concatenate([source[k, i, 16 * q:16 * q + 16, :] for k in range(4)], axis=0)
                wide = dot(pack, rows)
                moved = wide.astype(BF)
                for d in range(4):
                    target[place(i, 4 * q + d)] = moved[16 * d:16 * d + 16]
                if far is not None and q == 4:
                    edges[0].append(wide[0:8])
                if far is not None and q == 3:
                    edges[1].append(wide[56:64])
        if far is not None:
            for side in range(2):
                far[side] = jnp.concatenate(edges[side], axis=0).astype(BF)

    loads[0].wait()
    packed(obs, obs_out, lambda i, to: (to, i), far_out)
    obs_in[mem] = obs_out[mem]
    for load in loads[1:4]:
        load.wait()
    slot = iota((1, 128), 1)
    for i in range(2):
        for j in range(4):
            b = 4 * i + j
            weights[0, b:b + 1] = jnp.where(
                slot < counts[i, j], 1.0 / jnp.sqrt(variance[i, j:j + 1, :]), 0.0)
            weights[1, b:b + 1] = values[i, j:j + 1, :]

    @pl.when(tile == 0)
    def _():
        pl.semaphore_wait(barrier, mems)

    @pl.when(tile == tiles - 1)
    def _():
        pl.semaphore_wait(barrier, mems)

    @pl.when(jnp.logical_and(tile > 0, tile < tiles - 1))
    def _():
        pl.semaphore_wait(barrier, mems + 1)

    def send_all(source, target, send, receive, first, last):
        @pl.loop(first, last)
        def _(step):
            to = partner(step)
            pltpu.make_async_remote_copy(
                src_ref=source.at[to], dst_ref=target.at[mem], send_sem=send, recv_sem=receive,
                device_id={"mem": to}, device_id_type=MESH,
            ).start()

    def take(ref, semaphore):
        pltpu.make_async_copy(ref, ref, semaphore).wait()

    send_all(obs_out, obs_in, obs_s, obs_r, 16, 32)
    send_all(obs_out, obs_in, obs_s, obs_r, 1, 16)

    def to_middle(side):
        return pltpu.make_async_remote_copy(
            src_ref=far_out.at[side], dst_ref=far_in.at[mem], send_sem=far_s.at[side], recv_sem=far_r,
            device_id={"mem": middle + side}, device_id_type=MESH)

    def weights_over(side):
        return pltpu.make_async_remote_copy(
            src_ref=weights, dst_ref=far_weights, send_sem=weight_s, recv_sem=weight_r,
            device_id={"mem": middle + 1 - side}, device_id_type=MESH)

    for side in range(2):
        @pl.when(mem != middle + side)
        def _(side=side):
            to_middle(side).start()

        @pl.when(mem == middle + side)
        def _(side=side):
            weights_over(side).start()
            far_in[mem] = far_out[side]

    loads[4].wait()
    packed(state, state_out, lambda i, to: (i, to))
    for i in range(2):
        state_in[i, mem] = state_out[i, mem]
    r, c = iota((512, 512), 0), iota((512, 512), 1)
    perm[...] = one_hot(c == ((r // 4) % 32) * 16 + (r // 128) * 4 + r % 4)
    perm_back[...] = one_hot(r == ((c // 4) % 32) * 16 + (c // 128) * 4 + c % 4)

    some = pl.ds(0, mems - 1)
    take(obs_out.at[some], obs_s)
    take(obs_in.at[some], obs_r)

    def scale(member, given, b, col, i):
        mean = jnp.sum(member, axis=0, keepdims=True) * (1.0 / K)
        weight = given[0, b:b + 1]
        innovation = weight * (given[1, b:b + 1] - mean)
        scaled[col, i, 0:K] = ((member - mean) * weight).astype(BF)
        scaled[col, i, K:EXT] = jnp.where(
            iota((16, 128), 0) == 0, jnp.broadcast_to(innovation, (16, 128)), 0.0
        ).astype(BF)

    for i in range(2):
        wide = dot(perm[...], obs_in[:, i].reshape(512, 128))
        for j in range(4):
            scale(wide[128 * j:128 * j + 128], weights, 4 * i + j, j + 2, i)

    def to_left():
        return pltpu.make_async_remote_copy(
            src_ref=scaled.at[pl.ds(2, 2)], dst_ref=scaled.at[pl.ds(6, 2)], send_sem=col_s.at[0],
            recv_sem=col_r.at[0], device_id={"mem": mem - 1}, device_id_type=MESH)

    def to_right():
        return pltpu.make_async_remote_copy(
            src_ref=scaled.at[pl.ds(4, 2)], dst_ref=scaled.at[pl.ds(0, 2)], send_sem=col_s.at[1],
            recv_sem=col_r.at[1], device_id={"mem": mem + 1}, device_id_type=MESH)

    has_left = jnp.logical_and(mem != 0, mem != middle + 1)
    has_right = jnp.logical_and(mem != mems - 1, mem != middle)

    @pl.when(has_left)
    def _():
        to_left().start()

    @pl.when(has_right)
    def _():
        to_right().start()

    for side in range(2):
        @pl.when(mem == middle + side)
        def _(side=side):
            take(far_in.at[some], far_r)
            weights_over(side).wait()
            wide = dot(perm[...], far_in[...].reshape(512, 128))
            for i in range(2):
                for jj in range(2):
                    n = 2 * i + jj
                    scale(wide[128 * n:128 * n + 128], far_weights, 4 * i + 2 * side + jj, 6 - 6 * side + jj, i)

        @pl.when(mem != middle + side)
        def _(side=side):
            to_middle(side).wait_send()

    @pl.when(mem == 0)
    def _():
        scaled[0:2] = jnp.zeros((2, 2, EXT, 128), BF)

    @pl.when(mem == mems - 1)
    def _():
        scaled[6:8] = jnp.zeros((2, 2, EXT, 128), BF)

    def gram(col):
        for i in range(2):
            grams[col, i] = dot_t(scaled[col, i], scaled[col, i, 0:K])[:ROWS]

    def send_state(i, first, last):
        send_all(state_out.at[i], state_in.at[i], state_s.at[i], state_r.at[i], first, last)

    send_state(0, 16, 16 + FIRST)
    for col in range(2, 6):
        gram(col)

    @pl.when(has_left)
    def _():
        to_left().wait_send()
        to_right().wait_recv()

    @pl.when(has_right)
    def _():
        to_right().wait_send()
        to_left().wait_recv()

    for col in (0, 1, 6, 7):
        gram(col)
    for i in range(2):
        for j in range(4):
            total = NEAR[0] * grams[j, i]
            for b in range(1, 5):
                total = total + NEAR[b] * grams[j + b, i]
            sums[i, j] = total

    def to_above():
        return pltpu.make_async_remote_copy(
            src_ref=sums, dst_ref=below, send_sem=row_s.at[0], recv_sem=row_r.at[0],
            device_id={"tile": tile - 1}, device_id_type=MESH)

    def to_below():
        return pltpu.make_async_remote_copy(
            src_ref=sums, dst_ref=above, send_sem=row_s.at[1], recv_sem=row_r.at[1],
            device_id={"tile": tile + 1}, device_id_type=MESH)

    @pl.when(tile > 0)
    def _():
        to_above().start()

    @pl.when(tile < tiles - 1)
    def _():
        to_below().start()

    @pl.when(tile == 0)
    def _():
        above[...] = jnp.zeros(above.shape, F32)

    @pl.when(tile == tiles - 1)
    def _():
        below[...] = jnp.zeros(below.shape, F32)

    @pl.when(tile > 0)
    def _():
        to_above().wait_send()
        to_below().wait_recv()

    @pl.when(tile < tiles - 1)
    def _():
        to_below().wait_send()
        to_above().wait_recv()

    send_state(0, 16 + FIRST, 32)
    send_state(0, 1, 16)
    send_state(1, 16, 32)
    send_state(1, 1, 16)

    eye = jnp.where(iota((K, K), 0) == iota((K, K), 1), 1.0, 0.0).astype(F32)
    drives, norms = [], []
    for i in range(2):
        for j in range(4):
            b = 4 * i + j
            if i == 0:
                total = sums[0, j] + W1 * sums[1, j] + (W2 * above[0, j] + W1 * above[1, j]) + W2 * below[0, j]
            else:
                total = sums[1, j] + W1 * sums[0, j] + W2 * above[1, j] + (W1 * below[0, j] + W2 * below[1, j])
            system = total[:K] + (K - 1) * eye
            norm = jnp.sqrt(jnp.sum(jnp.sum(system * system, axis=1, keepdims=True), axis=0, keepdims=True))
            drives.append(total[K:ROWS])
            norms.append(norm)
            first = system / norm
            factor = 1.5 * eye - 0.5 * first
            right = right3(split3(factor))
            root[b] = mul3(mul3(first, right), right)
            inv[b] = factor

    for b in range(8):
        factor = 1.5 * eye - 0.5 * root[b]
        right = right3(split3(factor))
        inv[b] = mul3(inv[b], right)
        root[b] = mul3(mul3(root[b], right), right)

    @pl.loop(2, NS_ITERS - 1)
    def _(sweep):
        for b in range(8):
            factor = 1.5 * eye - 0.5 * root[b]
            right = right2(*split2(factor))
            inv[b] = mul2(inv[b], right)
            root[b] = mul2(mul2(root[b], right), right)

    for b in range(8):
        factor = 1.5 * eye - 0.5 * root[b]
        inverse = mul2(inv[b], right2(*split2(factor))) / jnp.sqrt(norms[b])
        right = right2(*split2(inverse))
        shift = mul2(mul2(drives[b], right), right)[0:1]
        mix[b] = (math.sqrt(K - 1) * inverse + shift).astype(BF)

    def send_result(i, first, last):
        send_all(res_out.at[i], res_in.at[i], res_s.at[i], res_r.at[i], first, last)

    for i in range(2):
        take(state_in.at[i, some], state_r.at[i])
        wide = dot(perm[...], state_in[i].reshape(512, 768))
        rows = []
        for j in range(4):
            member = wide[128 * j:128 * j + 128]
            mean = jnp.sum(member, axis=0, keepdims=True) * (1.0 / K)
            rows.append((mean + dot(mix[4 * i + j], (member - mean).astype(BF))).astype(BF))
        moved = dot(perm_back[...], jnp.concatenate(rows, axis=0)).astype(BF)
        res_out[i] = moved.reshape(32, 16, 768)
        send_result(i, 16, 32)
        send_result(i, 1, 16)
        res_in[i, mem] = res_out[i, mem]

    for i in range(2):
        take(res_in.at[i, some], res_r.at[i])
        for q in range(8):
            moved = dot(unpack, res_in[i, 4 * q:4 * q + 4].reshape(64, 768)).astype(BF)
            for k in range(4):
                out[i, k, 16 * q:16 * q + 16, :] = moved[16 * k:16 * k + 16]
        for k in range(4):
            pltpu.make_async_copy(out.at[i, k], out_hbm.at[k, i], store_s.at[i, k]).start()
        take(state_out.at[i, some], state_s.at[i])
        take(res_out.at[i, some], res_s.at[i])
    for i in range(2):
        for k in range(4):
            pltpu.make_async_copy(out.at[i, k], out_hbm.at[k, i], store_s.at[i, k]).wait()


def on_device(ensemble_state, obs_members, obs_values, obs_variance, obs_counts):
    hbm = pl.BlockSpec(memory_space=pl.ANY)
    dma, dmas = pltpu.SemaphoreType.DMA(()), pltpu.SemaphoreType.DMA((2,))
    obs_box, row_box = pltpu.VMEM((32, 2, 16, 128), BF), pltpu.VMEM((2, 32, 16, 768), BF)
    sum_box = pltpu.VMEM((2, 4, ROWS, 128), F32)
    square = pltpu.VMEM((8, K, K), F32)
    return pl.pallas_call(
        kernel,
        out_shape=jax.ShapeDtypeStruct(ensemble_state.shape, BF),
        in_specs=[hbm] * 5,
        out_specs=hbm,
        scratch_shapes=[
            pltpu.VMEM((4, 2, 128, 768), BF), pltpu.VMEM((4, 2, 128, 128), BF), pltpu.VMEM((2, 4, 128), F32),
            pltpu.VMEM((2, 4, 128), F32), pltpu.SMEM((2, 4), jnp.int32), pltpu.VMEM((2, 4, 128, 768), BF),
            obs_box, obs_box, row_box, row_box, row_box, row_box,
            pltpu.VMEM((2, 16, 128), BF), pltpu.VMEM((32, 16, 128), BF),
            pltpu.VMEM((2, 8, 128), F32), pltpu.VMEM((2, 8, 128), F32),
            pltpu.VMEM((8, 2, EXT, 128), BF), pltpu.VMEM((8, 2, ROWS, 128), F32),
            sum_box, sum_box, sum_box, square, square, pltpu.VMEM((8, K, K), BF),
            pltpu.VMEM((512, 512), BF), pltpu.VMEM((512, 512), BF),
            pltpu.SemaphoreType.DMA((5,)), pltpu.SemaphoreType.DMA((2, 4)), dmas, dma, dma, dma,
            dma, dma, dmas, dmas, dmas, dmas, dmas, dmas, dmas, dmas,
        ],
        compiler_params=pltpu.CompilerParams(
            collective_id=0, has_side_effects=True, vmem_limit_bytes=64 * 1024 * 1024
        ),
        cost_estimate=pl.CostEstimate(flops=10**10, bytes_accessed=4 * 10**6, transcendentals=0),
        name="letkf",
    )(ensemble_state, obs_members, obs_values, obs_variance, obs_counts)


def solution(mesh):
    placed = (
        P("mem", "tile", None, None),
        P("mem", "tile", None, None),
        P("tile", "mem", None),
        P("tile", "mem", None),
        P("tile", "mem"),
    )
    return jax.shard_map(
        on_device,
        mesh=mesh,
        in_specs=placed,
        out_specs=P("mem", "tile", None, None),
        check_vma=False,
    )
```

```python
import functools
import math

import jax
import jax.numpy as jnp
from jax import lax
from jax.experimental import pallas as pl
from jax.experimental.pallas import tpu as pltpu
from jax.sharding import PartitionSpec as P

NS_ITERS = 12
MESH = pl.DeviceIdType.MESH
BF = jnp.bfloat16
F32 = jnp.float32
W1 = math.exp(-0.25)
W2 = math.exp(-1.0)
NEAR = (W2, W1, 1.0, W1, W2)
K = 128
EXT = 144
ROWS = 136
FIRST = 4


def iota(shape, dim):
    return lax.broadcasted_iota(jnp.int32, shape, dim)


def dot(a, b):
    return lax.dot_general(a, b, (((1,), (0,)), ((), ())), preferred_element_type=F32)


def dot_t(a, b):
    return lax.dot_general(a, b, (((1,), (1,)), ((), ())), preferred_element_type=F32)


def one_hot(hit):
    return jnp.where(hit, 1.0, 0.0).astype(BF)


def split2(value):
    high = value.astype(BF)
    return high, (value - high.astype(F32)).astype(BF)


def split3(value):
    high = value.astype(BF)
    rest = value - high.astype(F32)
    mid = rest.astype(BF)
    return high, mid, (rest - mid.astype(F32)).astype(BF)


def right2(high, low):
    pair = jnp.concatenate([high, low], axis=1)
    return jnp.concatenate([pair, pair], axis=0)


def mul2(left, right):
    both = dot(jnp.concatenate(split2(left), axis=1), right)
    return both[:, :K] + both[:, K:]


def right3(parts):
    high, mid, low = parts
    return right2(high, mid), jnp.concatenate([high, low], axis=0)


def mul3(left, right):
    high, mid, low = split3(left)
    both = dot(jnp.concatenate([high, mid], axis=1), right[0])
    small = dot(jnp.concatenate([low, high], axis=1), right[1])
    return both[:, :K] + (both[:, K:] + small)


def kernel(
    state_hbm, obs_hbm, values_hbm, variance_hbm, counts_hbm, out_hbm,
    state, obs, values, variance, counts, out,
    obs_out, obs_in, state_out, state_in, res_out, res_in,
    far_out, far_in, weights, far_weights, scaled, grams, sums, above, below, root, inv, mix, perm, perm_back,
    load_s, store_s, far_s, far_r, weight_s, weight_r,
    obs_s, obs_r, state_s, state_r, col_s, col_r, row_s, row_r, res_s, res_r,
):
    mem, tile = lax.axis_index("mem"), lax.axis_index("tile")
    mems, tiles, middle = 32, 16, 15
    z, y, x = mem // 16, lax.rem(mem // 4, 4), lax.rem(mem, 4)

    def partner(step):
        pz = lax.rem(z + step // 16, 2)
        py = lax.rem(y + lax.rem(step // 4, 4), 4)
        px = lax.rem(x + lax.rem(step, 4), 4)
        return pz * 16 + py * 4 + px

    loads = [
        pltpu.make_async_copy(source, target, load_s.at[n]) for n, (source, target) in enumerate((
            (obs_hbm, obs), (values_hbm, values), (variance_hbm, variance), (counts_hbm, counts),
            (state_hbm, state)))
    ]
    for load in loads:
        load.start()
    barrier = pltpu.get_barrier_semaphore()

    @pl.loop(1, mems)
    def _(step):
        pl.semaphore_signal(barrier, inc=1, device_id={"mem": partner(step)}, device_id_type=MESH)

    @pl.when(tile > 0)
    def _():
        pl.semaphore_signal(barrier, inc=1, device_id={"tile": tile - 1}, device_id_type=MESH)

    @pl.when(tile < tiles - 1)
    def _():
        pl.semaphore_signal(barrier, inc=1, device_id={"tile": tile + 1}, device_id_type=MESH)

    r, c = iota((64, 64), 0), iota((64, 64), 1)
    pack = one_hot(c == (r % 4) * 16 + (r // 16) * 4 + (r // 4) % 4)
    unpack = one_hot(r == (c % 4) * 16 + (c // 16) * 4 + (c // 4) % 4)

    def packed(source, target, place, far=None):
        edges = ([], [])
        for i in range(2):
            for q in range(8):
                rows = jnp.concatenate([source[k, i, 16 * q:16 * q + 16, :] for k in range(4)], axis=0)
                wide = dot(pack, rows)
                moved = wide.astype(BF)
                for d in range(4):
                    target[place(i, 4 * q + d)] = moved[16 * d:16 * d + 16]
                if far is not None and q == 4:
                    edges[0].append(wide[0:8])
                if far is not None and q == 3:
                    edges[1].append(wide[56:64])
        if far is not None:
            for side in range(2):
                far[side] = jnp.concatenate(edges[side], axis=0).astype(BF)

    loads[0].wait()
    packed(obs, obs_out, lambda i, to: (to, i), far_out)
    obs_in[mem] = obs_out[mem]
    for load in loads[1:4]:
        load.wait()
    slot = iota((1, 128), 1)
    for i in range(2):
        for j in range(4):
            b = 4 * i + j
            weights[0, b:b + 1] = jnp.where(
                slot < counts[i, j], 1.0 / jnp.sqrt(variance[i, j:j + 1, :]), 0.0)
            weights[1, b:b + 1] = values[i, j:j + 1, :]

    @pl.when(tile == 0)
    def _():
        pl.semaphore_wait(barrier, mems)

    @pl.when(tile == tiles - 1)
    def _():
        pl.semaphore_wait(barrier, mems)

    @pl.when(jnp.logical_and(tile > 0, tile < tiles - 1))
    def _():
        pl.semaphore_wait(barrier, mems + 1)

    def send_all(source, target, send, receive, first, last):
        @pl.loop(first, last)
        def _(step):
            to = partner(step)
            pltpu.make_async_remote_copy(
                src_ref=source.at[to], dst_ref=target.at[mem], send_sem=send, recv_sem=receive,
                device_id={"mem": to}, device_id_type=MESH,
            ).start()

    def take(ref, semaphore):
        pltpu.make_async_copy(ref, ref, semaphore).wait()

    send_all(obs_out, obs_in, obs_s, obs_r, 16, 32)
    send_all(obs_out, obs_in, obs_s, obs_r, 1, 16)

    def to_middle(side):
        return pltpu.make_async_remote_copy(
            src_ref=far_out.at[side], dst_ref=far_in.at[mem], send_sem=far_s.at[side], recv_sem=far_r,
            device_id={"mem": middle + side}, device_id_type=MESH)

    def weights_over(side):
        return pltpu.make_async_remote_copy(
            src_ref=weights, dst_ref=far_weights, send_sem=weight_s, recv_sem=weight_r,
            device_id={"mem": middle + 1 - side}, device_id_type=MESH)

    for side in range(2):
        @pl.when(mem != middle + side)
        def _(side=side):
            to_middle(side).start()

        @pl.when(mem == middle + side)
        def _(side=side):
            weights_over(side).start()
            far_in[mem] = far_out[side]

    loads[4].wait()
    packed(state, state_out, lambda i, to: (i, to))
    for i in range(2):
        state_in[i, mem] = state_out[i, mem]
    r, c = iota((512, 512), 0), iota((512, 512), 1)
    perm[...] = one_hot(c == ((r // 4) % 32) * 16 + (r // 128) * 4 + r % 4)
    perm_back[...] = one_hot(r == ((c // 4) % 32) * 16 + (c // 128) * 4 + c % 4)

    some = pl.ds(0, mems - 1)
    def send_state(i, first, last):
        send_all(state_out.at[i], state_in.at[i], state_s.at[i], state_r.at[i], first, last)

    take(obs_out.at[some], obs_s)
    send_state(0, 1, 16)
    take(obs_in.at[some], obs_r)

    def scale(member, given, b, col, i):
        mean = jnp.sum(member, axis=0, keepdims=True) * (1.0 / K)
        weight = given[0, b:b + 1]
        innovation = weight * (given[1, b:b + 1] - mean)
        scaled[col, i, 0:K] = ((member - mean) * weight).astype(BF)
        scaled[col, i, K:EXT] = jnp.where(
            iota((16, 128), 0) == 0, jnp.broadcast_to(innovation, (16, 128)), 0.0
        ).astype(BF)

    for i in range(2):
        wide = dot(perm[...], obs_in[:, i].reshape(512, 128))
        for j in range(4):
            scale(wide[128 * j:128 * j + 128], weights, 4 * i + j, j + 2, i)

    def to_left():
        return pltpu.make_async_remote_copy(
            src_ref=scaled.at[pl.ds(2, 2)], dst_ref=scaled.at[pl.ds(6, 2)], send_sem=col_s.at[0],
            recv_sem=col_r.at[0], device_id={"mem": mem - 1}, device_id_type=MESH)

    def to_right():
        return pltpu.make_async_remote_copy(
            src_ref=scaled.at[pl.ds(4, 2)], dst_ref=scaled.at[pl.ds(0, 2)], send_sem=col_s.at[1],
            recv_sem=col_r.at[1], device_id={"mem": mem + 1}, device_id_type=MESH)

    has_left = jnp.logical_and(mem != 0, mem != middle + 1)
    has_right = jnp.logical_and(mem != mems - 1, mem != middle)

    @pl.when(has_left)
    def _():
        to_left().start()

    @pl.when(has_right)
    def _():
        to_right().start()

    for side in range(2):
        @pl.when(mem == middle + side)
        def _(side=side):
            take(far_in.at[some], far_r)
            weights_over(side).wait()
            wide = dot(perm[...], far_in[...].reshape(512, 128))
            for i in range(2):
                for jj in range(2):
                    n = 2 * i + jj
                    scale(wide[128 * n:128 * n + 128], far_weights, 4 * i + 2 * side + jj, 6 - 6 * side + jj, i)

        @pl.when(mem != middle + side)
        def _(side=side):
            to_middle(side).wait_send()

    @pl.when(mem == 0)
    def _():
        scaled[0:2] = jnp.zeros((2, 2, EXT, 128), BF)

    @pl.when(mem == mems - 1)
    def _():
        scaled[6:8] = jnp.zeros((2, 2, EXT, 128), BF)

    def gram(col):
        for i in range(2):
            grams[col, i] = dot_t(scaled[col, i], scaled[col, i, 0:K])[:ROWS]

    send_state(0, 16, 16 + FIRST)
    for col in range(2, 6):
        gram(col)

    @pl.when(has_left)
    def _():
        to_left().wait_send()
        to_right().wait_recv()

    @pl.when(has_right)
    def _():
        to_right().wait_send()
        to_left().wait_recv()

    for col in (0, 1, 6, 7):
        gram(col)
    for i in range(2):
        for j in range(4):
            total = NEAR[0] * grams[j, i]
            for b in range(1, 5):
                total = total + NEAR[b] * grams[j + b, i]
            sums[i, j] = total

    def to_above():
        return pltpu.make_async_remote_copy(
            src_ref=sums, dst_ref=below, send_sem=row_s.at[0], recv_sem=row_r.at[0],
            device_id={"tile": tile - 1}, device_id_type=MESH)

    def to_below():
        return pltpu.make_async_remote_copy(
            src_ref=sums, dst_ref=above, send_sem=row_s.at[1], recv_sem=row_r.at[1],
            device_id={"tile": tile + 1}, device_id_type=MESH)

    @pl.when(tile > 0)
    def _():
        to_above().start()

    @pl.when(tile < tiles - 1)
    def _():
        to_below().start()

    @pl.when(tile == 0)
    def _():
        above[...] = jnp.zeros(above.shape, F32)

    @pl.when(tile == tiles - 1)
    def _():
        below[...] = jnp.zeros(below.shape, F32)

    @pl.when(tile > 0)
    def _():
        to_above().wait_send()
        to_below().wait_recv()

    @pl.when(tile < tiles - 1)
    def _():
        to_below().wait_send()
        to_above().wait_recv()

    send_state(0, 16 + FIRST, 32)
    send_state(1, 16, 32)
    send_state(1, 1, 16)

    eye = jnp.where(iota((K, K), 0) == iota((K, K), 1), 1.0, 0.0).astype(F32)
    drives, norms = [], []
    for i in range(2):
        for j in range(4):
            b = 4 * i + j
            if i == 0:
                total = sums[0, j] + W1 * sums[1, j] + (W2 * above[0, j] + W1 * above[1, j]) + W2 * below[0, j]
            else:
                total = sums[1, j] + W1 * sums[0, j] + W2 * above[1, j] + (W1 * below[0, j] + W2 * below[1, j])
            system = total[:K] + (K - 1) * eye
            norm = jnp.sqrt(jnp.sum(jnp.sum(system * system, axis=1, keepdims=True), axis=0, keepdims=True))
            drives.append(total[K:ROWS])
            norms.append(norm)
            first = system / norm
            factor = 1.5 * eye - 0.5 * first
            right = right3(split3(factor))
            root[b] = mul3(mul3(first, right), right)
            inv[b] = factor

    for b in range(8):
        factor = 1.5 * eye - 0.5 * root[b]
        right = right3(split3(factor))
        inv[b] = mul3(inv[b], right)
        root[b] = mul3(mul3(root[b], right), right)

    @pl.loop(2, NS_ITERS - 1)
    def _(sweep):
        for b in range(8):
            factor = 1.5 * eye - 0.5 * root[b]
            right = right2(*split2(factor))
            inv[b] = mul2(inv[b], right)
            root[b] = mul2(mul2(root[b], right), right)

    for b in range(8):
        factor = 1.5 * eye - 0.5 * root[b]
        inverse = mul2(inv[b], right2(*split2(factor))) / jnp.sqrt(norms[b])
        right = right2(*split2(inverse))
        shift = mul2(mul2(drives[b], right), right)[0:1]
        mix[b] = (math.sqrt(K - 1) * inverse + shift).astype(BF)

    def send_result(i, first, last):
        send_all(res_out.at[i], res_in.at[i], res_s.at[i], res_r.at[i], first, last)

    for i in range(2):
        take(state_in.at[i, some], state_r.at[i])
        wide = dot(perm[...], state_in[i].reshape(512, 768))
        rows = []
        for j in range(4):
            member = wide[128 * j:128 * j + 128]
            mean = jnp.sum(member, axis=0, keepdims=True) * (1.0 / K)
            rows.append((mean + dot(mix[4 * i + j], (member - mean).astype(BF))).astype(BF))
        moved = dot(perm_back[...], jnp.concatenate(rows, axis=0)).astype(BF)
        res_out[i] = moved.reshape(32, 16, 768)
        send_result(i, 16, 32)
        send_result(i, 1, 16)
        res_in[i, mem] = res_out[i, mem]

    for i in range(2):
        take(res_in.at[i, some], res_r.at[i])
        for q in range(8):
            moved = dot(unpack, res_in[i, 4 * q:4 * q + 4].reshape(64, 768)).astype(BF)
            for k in range(4):
                out[i, k, 16 * q:16 * q + 16, :] = moved[16 * k:16 * k + 16]
        for k in range(4):
            pltpu.make_async_copy(out.at[i, k], out_hbm.at[k, i], store_s.at[i, k]).start()
        take(state_out.at[i, some], state_s.at[i])
        take(res_out.at[i, some], res_s.at[i])
    for i in range(2):
        for k in range(4):
            pltpu.make_async_copy(out.at[i, k], out_hbm.at[k, i], store_s.at[i, k]).wait()


def on_device(ensemble_state, obs_members, obs_values, obs_variance, obs_counts):
    hbm = pl.BlockSpec(memory_space=pl.ANY)
    dma, dmas = pltpu.SemaphoreType.DMA(()), pltpu.SemaphoreType.DMA((2,))
    obs_box, row_box = pltpu.VMEM((32, 2, 16, 128), BF), pltpu.VMEM((2, 32, 16, 768), BF)
    sum_box = pltpu.VMEM((2, 4, ROWS, 128), F32)
    square = pltpu.VMEM((8, K, K), F32)
    return pl.pallas_call(
        kernel,
        out_shape=jax.ShapeDtypeStruct(ensemble_state.shape, BF),
        in_specs=[hbm] * 5,
        out_specs=hbm,
        scratch_shapes=[
            pltpu.VMEM((4, 2, 128, 768), BF), pltpu.VMEM((4, 2, 128, 128), BF), pltpu.VMEM((2, 4, 128), F32),
            pltpu.VMEM((2, 4, 128), F32), pltpu.SMEM((2, 4), jnp.int32), pltpu.VMEM((2, 4, 128, 768), BF),
            obs_box, obs_box, row_box, row_box, row_box, row_box,
            pltpu.VMEM((2, 16, 128), BF), pltpu.VMEM((32, 16, 128), BF),
            pltpu.VMEM((2, 8, 128), F32), pltpu.VMEM((2, 8, 128), F32),
            pltpu.VMEM((8, 2, EXT, 128), BF), pltpu.VMEM((8, 2, ROWS, 128), F32),
            sum_box, sum_box, sum_box, square, square, pltpu.VMEM((8, K, K), BF),
            pltpu.VMEM((512, 512), BF), pltpu.VMEM((512, 512), BF),
            pltpu.SemaphoreType.DMA((5,)), pltpu.SemaphoreType.DMA((2, 4)), dmas, dma, dma, dma,
            dma, dma, dmas, dmas, dmas, dmas, dmas, dmas, dmas, dmas,
        ],
        compiler_params=pltpu.CompilerParams(
            collective_id=0, has_side_effects=True, vmem_limit_bytes=64 * 1024 * 1024
        ),
        cost_estimate=pl.CostEstimate(flops=10**10, bytes_accessed=4 * 10**6, transcendentals=0),
        name="letkf",
    )(ensemble_state, obs_members, obs_values, obs_variance, obs_counts)


def solution(mesh):
    placed = (
        P("mem", "tile", None, None),
        P("mem", "tile", None, None),
        P("tile", "mem", None),
        P("tile", "mem", None),
        P("tile", "mem"),
    )
    return jax.shard_map(
        on_device,
        mesh=mesh,
        in_specs=placed,
        out_specs=P("mem", "tile", None, None),
        check_vma=False,
    )
```
